512 devices in a mesh: fsdp: 128 (over z, y, core), rep: 4 (over x).
Axes of the slice: x: 4, y: 8, z: 8, core: 2. Of those that a mesh axis runs over, the one named last changes fastest.
Arguments:
- grads: float32 [4, 128, 72, 4, 1024], P('rep', 'fsdp'), may hold values from -4 to 4
- momentum: float32 [128, 72, 4, 1024], P('fsdp'), may hold values from -6 to 6
- lengths: int32 [72, 128], replicated, may hold values from 1 to 4, 384 in all within a row
- owner: int32 [72], replicated, may hold values from 0 to 127, as said below
Outputs:
- new_momentum: float32 [128, 72, 4, 1024], P('fsdp')
- update: bfloat16 [128, 72, 4, 1024], P('fsdp')
- owned: bfloat16 [128, 384, 1024], P('fsdp')
The draws below stay inside these ranges and needn't reach their ends.
Inputs may be any that keep to these rules, and one draw needn't show every extreme that they name: Row m of lengths adds up to 384, and one of its entries is exactly 4. `owner`: the owners of different matrices are different devices.
All inputs are finite; a program needn't handle non-finite values.
Results may differ from the reference program's by a relative error of at most 0.035.
Values may be sent and summed in bfloat16 or wider, within the bound.
No kernel may reach another device: no remote copies, remote signals or barrier semaphores. Data moves between devices by JAX's collectives and lax.ppermute only.
A program may use at most 64 MiB of HBM per device.

```python
import math
import jax
import jax.numpy as jnp
import numpy as np
from jax import lax

R = 384
C = 1024
ITERS = 5
M = 72
PMAX = 4
N_FSDP = 128
N_REP = 4


def draw_owner(key, part):
    key = jax.random.fold_in(key, 7)
    middle_key = jax.random.fold_in(key, 1)
    order_key = jax.random.fold_in(key, 2)
    middle = jax.random.permutation(middle_key, N_FSDP - 2)[:M - 2].astype(jnp.int32) + 1
    chosen = jnp.concatenate([jnp.array([0, N_FSDP - 1], jnp.int32), middle])
    return jax.random.permutation(order_key, chosen).astype(jnp.int32)


def block_levels(own_key, shape, cuts, least, largest):
    def one(position, blocks):
        draws = jax.random.uniform(jax.random.fold_in(jax.random.fold_in(own_key, 6), position), (blocks,), jnp.float32, least / len(cuts), largest / len(cuts))
        return jnp.repeat(jnp.exp(draws), shape[position] // blocks).reshape((-1,) + (1,) * (len(shape) - position - 1))

    gain = one(*cuts[0])
    for cut in cuts[1:]:
        gain = gain * one(*cut)
    return gain


def profile(number_of, total, reach, slope):
    portions = [(1 << 20) // math.isqrt(rank ** slope) + 1 for rank in range(2, number_of + 1)]
    surplus, holding = total - reach - (number_of - 1), [1] * (number_of - 1)
    while surplus > 0:
        candidates = [i for i in range(number_of - 1) if holding[i] < reach]
        mass, remaining = sum([portions[i] for i in candidates]), surplus
        for i in candidates:
            extra = min(reach - holding[i], max(1, remaining * portions[i] // mass), surplus)
            holding[i] = holding[i] + extra
            surplus = surplus - extra
    return np.array([reach] + holding)


def ragged_sizes(rng, number_of, total, limit, slope):
    if number_of == 2:
        one = jax.random.randint(rng, (), max(1, total - limit), min(limit, total - 1) + 1)
        return jnp.stack([one, total - one])
    sizes = jnp.asarray(profile(number_of, total, limit, slope), jnp.int32)
    twos = (number_of - 1) // 2
    source_of, receiver = sizes[1:1 + 2 * twos:2], sizes[2:2 + 2 * twos:2]
    room = jnp.minimum(source_of - 1, limit - receiver)
    moved = jax.random.randint(jax.random.fold_in(rng, 1), (twos,), 0, 1 << 20) % (room + 1)
    sizes = sizes.at[1:1 + 2 * twos:2].set(source_of - moved).at[2:2 + 2 * twos:2].set(receiver + moved)
    return sizes[jax.random.permutation(jax.random.fold_in(rng, 2), number_of)]


def normal_values(own_key, shape, spread, reach, split=(), kind=jnp.bfloat16):
    drawn = jax.random.normal(own_key, shape, jnp.float32) * spread
    if len(split) > 0:
        drawn = block_levels(own_key, shape, split, -0.22, 0.18) * drawn
    return jnp.clip(drawn, min=-reach, max=reach).astype(kind)


def setup_inputs(seed: int = 0) -> dict:
    key_list = jax.random.split(jax.random.key(seed), 5)
    return {
        "grads": normal_values(key_list[0], (N_REP, N_FSDP, M, PMAX, C), 0.5, 4.0, ((0, 4), (1, 128)), jnp.float32),
        "momentum": normal_values(key_list[1], (N_FSDP, M, PMAX, C), 1.0, 6.0, ((0, 128),), jnp.float32),
        "lengths": jax.vmap(lambda own: ragged_sizes(own, N_FSDP, R, PMAX, 2))(jax.random.split(key_list[2], M)).reshape((M, N_FSDP)).astype(jnp.int32),
        "owner": draw_owner(jax.random.fold_in(key_list[4], 71), 0),
    }


COEF_A = 3.4445
COEF_B = -4.775
COEF_C = 2.0315

def newton_schulz(matrix):
    norm_value = jnp.sqrt(jnp.sum(matrix * matrix))
    iterate = (matrix / (norm_value + 1e-07)).astype(jnp.bfloat16)
    for step_index in range(ITERS):
        gram = jnp.dot(iterate, iterate.T, preferred_element_type=jnp.float32).astype(jnp.bfloat16)
        square = jnp.dot(gram, gram, preferred_element_type=jnp.float32)
        poly = (COEF_B * gram.astype(jnp.float32) + COEF_C * square).astype(jnp.bfloat16)
        iterate = (COEF_A * iterate.astype(jnp.float32) + jnp.dot(poly, iterate, preferred_element_type=jnp.float32)).astype(jnp.bfloat16)
    return -math.sqrt(max(R, C)) * iterate.astype(jnp.float32)

def reference(grads, momentum, lengths, owner):
    total = lax.optimization_barrier(jnp.sum(grads, axis=0))
    slot_ids = jnp.arange(PMAX, dtype=jnp.int32)
    lens_dev = lengths.T
    live = slot_ids[None, None, :] < lens_dev[:, :, None]
    new_momentum = jnp.where(live[..., None], 0.95 * momentum + total, jnp.float32(0.0))
    offsets = jnp.cumsum(lengths, axis=1).astype(jnp.int32) - lengths
    row_ids = jnp.arange(R, dtype=jnp.int32)

    def orthogonal(index):
        lens_row = lax.dynamic_slice_in_dim(lengths, index, 1, 0)[0]
        inclusive = jnp.cumsum(lens_row).astype(jnp.int32)
        starts = inclusive - lens_row
        source = lax.optimization_barrier(jnp.sum((inclusive[None, :] <= row_ids[:, None]).astype(jnp.int32), axis=1)).astype(jnp.int32)
        local = row_ids - starts[source]
        column = lax.dynamic_slice_in_dim(new_momentum, index, 1, 1)[:, 0]
        flat_rows = column.reshape(N_FSDP * PMAX, C)
        return newton_schulz(flat_rows[source * PMAX + local])
    updates = lax.map(orthogonal, jnp.arange(M, dtype=jnp.int32))
    owned = jnp.zeros((N_FSDP, R, C), jnp.bfloat16).at[owner].set(updates.astype(jnp.bfloat16))
    row_index = jnp.clip(offsets.T[:, :, None] + slot_ids[None, None, :], 0, R - 1)
    matrix_index = jnp.arange(M, dtype=jnp.int32)[None, :, None]
    pieces = updates[matrix_index, row_index]
    update = jnp.where(live[..., None], pieces, jnp.float32(0.0)).astype(jnp.bfloat16)
    return (new_momentum, update, owned)
```

```python
import functools
import math

import jax
import jax.numpy as jnp
from jax import lax
from jax.experimental import pallas as pl
from jax.experimental.pallas import tpu as pltpu
from jax.sharding import PartitionSpec as P

R = 384
ITERS = 5

COEF_A = 3.4445
COEF_B = -4.775
COEF_C = 2.0315

LANES = 128
ROWS = 8
BF16 = jnp.bfloat16
F32 = jnp.float32
VMEM_LIMIT = 48 * 1024 * 1024


def vmem():
    return pl.BlockSpec(memory_space=pltpu.VMEM)


def hbm():
    return pl.BlockSpec(memory_space=pltpu.HBM)


def later():
    return pl.BlockSpec(memory_space=pl.ANY)


def smem():
    return pl.BlockSpec(memory_space=pltpu.SMEM)


def params(limit=VMEM_LIMIT):
    return pltpu.CompilerParams(vmem_limit_bytes=limit)


def cost(flops, nbytes):
    return pl.CostEstimate(flops=flops, bytes_accessed=nbytes, transcendentals=0)


def column_of(half, block):
    if isinstance(block, int):
        return block * 2 * LANES + half * LANES
    return pl.multiple_of(block * (2 * LANES) + half * LANES, LANES)


def to_rows(src_ref, block, scratch):
    slots = src_ref.shape[1]
    for half in range(2):
        scratch[:, half * slots:(half + 1) * slots, :] = src_ref[:, :, pl.ds(column_of(half, block), LANES)]
    return scratch[...].reshape(scratch.shape[0] * ROWS, LANES)


def split_kernel(g_ref, out_ref, arrived, scratch, packed, in_sems, out_sems):
    blocks = out_ref.shape[0]
    wide = 2 * LANES
    reads = [
        pltpu.make_async_copy(g_ref.at[:, :, block * wide:(block + 1) * wide], arrived.at[block], in_sems.at[block])
        for block in range(blocks)
    ]
    writes = [pltpu.make_async_copy(packed.at[block], out_ref.at[block], out_sems.at[block]) for block in range(blocks)]
    for read in reads:
        read.start()
    for block in range(blocks):
        reads[block].wait()
        packed[block] = to_rows(arrived.at[block], 0, scratch.at[block]).astype(BF16)
        writes[block].start()
    for write in writes:
        write.wait()


def own_kernel(owner_ref, lens_ref, mom_ref, base_ref, pick_ref, place_ref, scratch):
    base_ref[...] = 0.95 * to_rows(mom_ref, lax.axis_index("rep"), scratch)
    pick_kernel(owner_ref, lens_ref, pick_ref, place_ref)


def scatter_kernel(owner_ref, base_ref, parts_ref, send_ref, tot_ref, packed):
    reps = parts_ref.shape[0]
    total = parts_ref[0].astype(F32)
    for rep in range(1, reps):
        total = total + parts_ref[rep].astype(F32)
    tot_ref[...] = total.astype(BF16)
    nm = base_ref[...] + total
    packed[...] = jnp.zeros_like(packed)
    for m in range(nm.shape[0] // ROWS):
        at = pl.multiple_of(owner_ref[m] * ROWS, ROWS)
        packed[pl.ds(at, ROWS), :] = nm[m * ROWS:(m + 1) * ROWS, :]
    send_ref[...] = packed[...].astype(BF16)


def pick_kernel(owner_ref, lens_ref, pick_ref, place_ref):
    me = lax.axis_index("fsdp")
    rows, slots8 = pick_ref.shape
    count = lens_ref.shape[1]

    def find(m, found):
        return jnp.where(owner_ref[m] == me, m, found)

    mine = lax.fori_loop(0, lens_ref.shape[0], find, -1)
    lens = lens_ref[pl.ds(jnp.maximum(mine, 0), 1), :]
    lens = jnp.where(mine >= 0, lens, 0).astype(F32)
    many = jnp.broadcast_to(lens, (LANES, count)).astype(BF16)

    def table(shape, slot_dim, before):
        device = lax.broadcasted_iota(jnp.int32, shape, 1 - slot_dim)
        source = lax.broadcasted_iota(jnp.int32, shape, slot_dim) // ROWS
        hit = device < source if before else device == source
        return jnp.where(hit, F32(1.0), F32(0.0)).astype(BF16)

    def source_row(shape, slot_dim, start, length):
        slot = (lax.broadcasted_iota(jnp.int32, shape, slot_dim) % 4)
        return jnp.where(slot < length.astype(jnp.int32), start.astype(jnp.int32) + slot, -1)

    few = many[:16, :]
    start = jnp.dot(few, table((count, slots8), 1, True), preferred_element_type=F32)[:8]
    length = jnp.dot(few, table((count, slots8), 1, False), preferred_element_type=F32)[:8]
    source = source_row((8, slots8), 1, start, length)[:1]
    hit = lax.broadcasted_iota(jnp.int32, (rows, slots8), 0) == source
    pick_ref[...] = jnp.where(hit, F32(1.0), F32(0.0)).astype(BF16)

    contract = (((1,), (1,)), ((), ()))
    start = lax.dot_general(table((slots8, count), 0, True), many, contract, preferred_element_type=F32)
    length = lax.dot_general(table((slots8, count), 0, False), many, contract, preferred_element_type=F32)
    source = source_row((slots8, LANES), 0, start, length)
    for at in range(0, rows, LANES):
        some = min(LANES, rows - at)
        hit = lax.broadcasted_iota(jnp.int32, (slots8, some), 1) + at == source[:, :some]
        place_ref[:, at:at + some] = jnp.where(hit, F32(1.0), F32(0.0)).astype(BF16)


def in_half(shape, half):
    return (lax.broadcasted_iota(jnp.int32, shape, 0) // 4) % 2 == half


def compact_kernel(pick_ref, in_ref, _, out_ref):
    slots8 = pick_ref.shape[1]
    upper = in_half((slots8, LANES), 0)
    got = in_ref[...].astype(F32)
    both = jnp.concatenate([jnp.where(upper, got, 0.0), jnp.where(upper, 0.0, got)], axis=1).astype(BF16)
    picked = jnp.dot(pick_ref[...], both, preferred_element_type=F32).astype(BF16)
    for rep in range(out_ref.shape[0]):
        out_ref[rep] = picked


def newton_schulz_kernel(scale, place_ref, pieces_ref, total_ref, first_ref, owned_ref, back_ref, joined_ref, matrix, x):
    rows8 = total_ref.shape[0]
    joined_ref[:rows8, :] = total_ref[...]
    joined_ref[rows8:, :] = first_ref[...]
    me = lax.axis_index("rep")
    wide = 2 * LANES
    upper = in_half((place_ref.shape[0], LANES), 0)
    for block in range(pieces_ref.shape[0]):
        matrix[:, block * wide:(block + 1) * wide] = pieces_ref[block].astype(F32)
    squares = jnp.sum(matrix[...] * matrix[...])
    factor = 1.0 / (jnp.sqrt(jnp.full((1, LANES), squares, F32)) + 1e-07)
    for tile in range(matrix.shape[1] // LANES):
        at = slice(tile * LANES, (tile + 1) * LANES)
        x[:, at] = (matrix[:, at] * factor).astype(BF16)

    def step(index, carry):
        contract = (((1,), (1,)), ((), ()))
        gram = lax.dot_general(x[...], x[...], contract, preferred_element_type=F32).astype(BF16)
        square = jnp.dot(gram, gram, preferred_element_type=F32)
        poly = (COEF_B * gram.astype(F32) + COEF_C * square).astype(BF16)
        for tile in range(x.shape[1] // wide):
            at = slice(tile * wide, (tile + 1) * wide)
            part = x[:, at]
            x[:, at] = (COEF_A * part.astype(F32) + jnp.dot(poly, part, preferred_element_type=F32)).astype(BF16)
        return carry

    lax.fori_loop(0, ITERS, step, 0)
    owned_ref[...] = (-scale * x[...].astype(F32)).astype(BF16)
    mine = owned_ref[:, pl.ds(column_of(0, me), wide)]
    spread = jnp.dot(place_ref[...], mine, preferred_element_type=F32)
    back_ref[...] = jnp.where(upper, spread[:, :LANES], spread[:, LANES:]).astype(BF16)


def select_kernel(owner_ref, back_ref, _, out_ref, wide, chosen):
    wide[...] = back_ref[...].astype(F32)
    for m in range(chosen.shape[0] // ROWS):
        at = pl.multiple_of(owner_ref[m] * ROWS, ROWS)
        chosen[m * ROWS:(m + 1) * ROWS, :] = wide[pl.ds(at, ROWS), :]
    rounded = chosen[...].astype(BF16)
    for rep in range(out_ref.shape[0]):
        out_ref[rep] = rounded


def partners():
    core = lax.rem(lax.axis_index("fsdp"), 2)
    return 1 + 2 * core, 3 - 2 * core


def blocks_of(own_ref, first_ref, second_ref):
    me = lax.axis_index("rep")
    first, second = partners()
    rows = own_ref.shape[0]
    return (
        (me, own_ref),
        (me ^ first, first_ref),
        (me ^ second, second_ref.at[:rows]),
        (me ^ 2, second_ref.at[rows:]),
    )


def columns(blocks, count):
    slots = ROWS // 2
    for block, piece in blocks:
        got = piece[...].astype(F32).reshape(count, ROWS, LANES)
        for half in range(2):
            yield pl.ds(column_of(half, block), LANES), got[:, half * slots:(half + 1) * slots, :]


def update_kernel(pieces_ref, out_ref):
    for at, got in columns([(block, pieces_ref.at[block]) for block in range(pieces_ref.shape[0])], out_ref.shape[0]):
        out_ref[:, :, at] = got.astype(BF16)


def momentum_kernel(lens_ref, mom_ref, own_ref, first_ref, second_ref, out_ref, done_ref, total):
    done_ref[...] = jnp.zeros_like(done_ref)
    device = lax.axis_index("fsdp")
    count, slots, width = out_ref.shape
    for at, got in columns(blocks_of(own_ref, first_ref, second_ref), count):
        total[:, :, at] = got
    slot = lax.broadcasted_iota(jnp.int32, (slots, width), 0)
    for m in range(count):
        live = slot < lens_ref[m, device]
        out_ref[m] = jnp.where(live, 0.95 * mom_ref[m] + total[m], 0.0)


def swap(value, step):
    devices, reps = lax.axis_size("fsdp"), lax.axis_size("rep")
    pairs = []
    for device in range(devices):
        flip = (1, 3)[(device + step) % 2]
        pairs += [(device * reps + rep, device * reps + (rep ^ flip)) for rep in range(reps)]
    return lax.ppermute(value, ("fsdp", "rep"), pairs)


def exchange(value):
    flat = value.reshape((value.shape[0] * value.shape[1],) + value.shape[2:])
    return lax.all_to_all(flat, "rep", split_axis=0, concat_axis=0, tiled=True).reshape(value.shape)


def body(grads, momentum, lengths, owner):
    reps = lax.axis_size("rep")
    devices = lax.axis_size("fsdp")
    count, slots, width = momentum.shape[1:]
    g, mom = grads[0, 0], momentum[0]
    rows8, slots8 = count * ROWS, devices * ROWS
    shape = jax.ShapeDtypeStruct
    part = shape((rows8, LANES), BF16)
    parts = shape((reps, rows8, LANES), BF16)

    split = pl.pallas_call(
        split_kernel,
        out_shape=parts,
        in_specs=[hbm()],
        out_specs=hbm(),
        scratch_shapes=[
            pltpu.VMEM((reps, count, slots, 2 * LANES), F32),
            pltpu.VMEM((reps, count, ROWS, LANES), F32),
            pltpu.VMEM((reps, rows8, LANES), BF16),
            pltpu.SemaphoreType.DMA((reps,)),
            pltpu.SemaphoreType.DMA((reps,)),
        ],
        compiler_params=params(60 * 1024 * 1024),
        cost_estimate=cost(0, 2_000_000),
        name="split",
    )(g)
    got = exchange(split)
    base, pick, place = pl.pallas_call(
        own_kernel,
        out_shape=[shape((rows8, LANES), F32), shape((R, slots8), BF16), shape((slots8, R), BF16)],
        in_specs=[smem()] + [vmem()] * 2,
        out_specs=[vmem()] * 3,
        scratch_shapes=[pltpu.VMEM((count, ROWS, LANES), F32)],
        compiler_params=params(),
        cost_estimate=cost(0, 4_000_000),
        name="own",
    )(owner, lengths, mom)
    send, total = pl.pallas_call(
        scatter_kernel,
        out_shape=[shape((slots8, LANES), BF16), part],
        in_specs=[smem(), vmem(), vmem()],
        out_specs=[vmem()] * 2,
        scratch_shapes=[pltpu.VMEM((slots8, LANES), F32)],
        compiler_params=params(),
        cost_estimate=cost(0, 2_000_000),
        name="scatter",
    )(owner, base, got)
    first = swap(total, 0)
    incoming = lax.all_to_all(send, "fsdp", split_axis=0, concat_axis=0, tiled=True)
    compact = pl.pallas_call(
        compact_kernel,
        out_shape=shape((reps, R, 2 * LANES), BF16),
        in_specs=[vmem()] * 2 + [later()],
        out_specs=vmem(),
        compiler_params=params(),
        cost_estimate=cost(200_000_000, 2_000_000),
        name="compact",
    )(pick, incoming, first)

    pieces = exchange(compact)
    owned, back, joined = pl.pallas_call(
        functools.partial(newton_schulz_kernel, math.sqrt(max(R, width))),
        out_shape=[shape((R, width), BF16), shape((slots8, LANES), BF16), shape((2 * rows8, LANES), BF16)],
        in_specs=[vmem()] * 4,
        out_specs=[vmem()] * 3,
        scratch_shapes=[pltpu.VMEM((R, width), F32), pltpu.VMEM((R, width), BF16)],
        compiler_params=params(),
        cost_estimate=cost(5_000_000_000, 4_000_000),
        name="newton_schulz",
    )(place, pieces, total, first)
    returned = lax.all_to_all(back, "fsdp", split_axis=0, concat_axis=0, tiled=True)
    new_momentum, done = pl.pallas_call(
        momentum_kernel,
        out_shape=[shape((count, slots, width), F32), shape((8, LANES), F32)],
        in_specs=[smem()] + [vmem()] * 4,
        out_specs=[vmem()] * 2,
        scratch_shapes=[pltpu.VMEM((count, slots, width), F32)],
        compiler_params=params(),
        cost_estimate=cost(0, 4_000_000),
        name="momentum",
    )(lengths, mom, total, first, swap(joined, 1))
    chosen = pl.pallas_call(
        select_kernel,
        out_shape=parts,
        in_specs=[smem(), vmem(), later()],
        out_specs=vmem(),
        scratch_shapes=[pltpu.VMEM((slots8, LANES), F32), pltpu.VMEM((rows8, LANES), F32)],
        compiler_params=params(),
        cost_estimate=cost(0, 1_000_000),
        name="select",
    )(owner, returned, done)
    update = pl.pallas_call(
        update_kernel,
        out_shape=shape((count, slots, width), BF16),
        in_specs=[vmem()],
        out_specs=vmem(),
        compiler_params=params(),
        cost_estimate=cost(0, 2_000_000),
        name="update",
    )(exchange(chosen))
    return (new_momentum[None], update[None], owned[None])


def solution(mesh):
    in_specs = (P("rep", "fsdp", None, None, None), P("fsdp", None, None, None), P(), P())
    out_specs = (P("fsdp", None, None, None), P("fsdp", None, None, None), P("fsdp", None, None))
    return jax.shard_map(body, mesh=mesh, in_specs=in_specs, out_specs=out_specs, check_vma=False)
```

```python
import functools
import math

import jax
import jax.numpy as jnp
from jax import lax
from jax.experimental import pallas as pl
from jax.experimental.pallas import tpu as pltpu
from jax.sharding import PartitionSpec as P

R = 384
ITERS = 5

COEF_A = 3.4445
COEF_B = -4.775
COEF_C = 2.0315

LANES = 128
ROWS = 8
BF16 = jnp.bfloat16
F32 = jnp.float32
VMEM_LIMIT = 48 * 1024 * 1024


def vmem():
    return pl.BlockSpec(memory_space=pltpu.VMEM)


def hbm():
    return pl.BlockSpec(memory_space=pltpu.HBM)


def later():
    return pl.BlockSpec(memory_space=pl.ANY)


def smem():
    return pl.BlockSpec(memory_space=pltpu.SMEM)


def params(limit=VMEM_LIMIT):
    return pltpu.CompilerParams(vmem_limit_bytes=limit)


def cost(flops, nbytes):
    return pl.CostEstimate(flops=flops, bytes_accessed=nbytes, transcendentals=0)


def column_of(half, block):
    if isinstance(block, int):
        return block * 2 * LANES + half * LANES
    return pl.multiple_of(block * (2 * LANES) + half * LANES, LANES)


def to_rows(src_ref, block, scratch):
    slots = src_ref.shape[1]
    for half in range(2):
        scratch[:, half * slots:(half + 1) * slots, :] = src_ref[:, :, pl.ds(column_of(half, block), LANES)]
    return scratch[...].reshape(scratch.shape[0] * ROWS, LANES)


def split_kernel(g_ref, out_ref, arrived, scratch, packed, in_sems, out_sems):
    blocks = out_ref.shape[0]
    wide = 2 * LANES
    reads = [
        pltpu.make_async_copy(g_ref.at[:, :, block * wide:(block + 1) * wide], arrived.at[block], in_sems.at[block])
        for block in range(blocks)
    ]
    writes = [pltpu.make_async_copy(packed.at[block], out_ref.at[block], out_sems.at[block]) for block in range(blocks)]
    for read in reads:
        read.start()
    for block in range(blocks):
        reads[block].wait()
        packed[block] = to_rows(arrived.at[block], 0, scratch.at[block]).astype(BF16)
        writes[block].start()
    for write in writes:
        write.wait()


def own_kernel(owner_ref, lens_ref, mom_ref, base_ref, pick_ref, place_ref, scratch):
    base_ref[...] = 0.95 * to_rows(mom_ref, lax.axis_index("rep"), scratch)
    pick_kernel(owner_ref, lens_ref, pick_ref, place_ref)


def scatter_kernel(owner_ref, base_ref, parts_ref, send_ref, tot_ref, packed):
    reps = parts_ref.shape[0]
    total = parts_ref[0].astype(F32)
    for rep in range(1, reps):
        total = total + parts_ref[rep].astype(F32)
    tot_ref[...] = total.astype(BF16)
    nm = base_ref[...] + total
    packed[...] = jnp.zeros_like(packed)
    for m in range(nm.shape[0] // ROWS):
        at = pl.multiple_of(owner_ref[m] * ROWS, ROWS)
        packed[pl.ds(at, ROWS), :] = nm[m * ROWS:(m + 1) * ROWS, :]
    send_ref[...] = packed[...].astype(BF16)


def pick_kernel(owner_ref, lens_ref, pick_ref, place_ref):
    me = lax.axis_index("fsdp")
    rows, slots8 = pick_ref.shape
    count = lens_ref.shape[1]

    def find(m, found):
        return jnp.where(owner_ref[m] == me, m, found)

    mine = lax.fori_loop(0, lens_ref.shape[0], find, -1)
    lens = lens_ref[pl.ds(jnp.maximum(mine, 0), 1), :]
    lens = jnp.where(mine >= 0, lens, 0).astype(F32)
    many = jnp.broadcast_to(lens, (LANES, count)).astype(BF16)

    def table(shape, slot_dim, before):
        device = lax.broadcasted_iota(jnp.int32, shape, 1 - slot_dim)
        source = lax.broadcasted_iota(jnp.int32, shape, slot_dim) // ROWS
        hit = device < source if before else device == source
        return jnp.where(hit, F32(1.0), F32(0.0)).astype(BF16)

    def source_row(shape, slot_dim, start, length):
        slot = (lax.broadcasted_iota(jnp.int32, shape, slot_dim) % 4)
        return jnp.where(slot < length.astype(jnp.int32), start.astype(jnp.int32) + slot, -1)

    few = many[:16, :]
    start = jnp.dot(few, table((count, slots8), 1, True), preferred_element_type=F32)[:8]
    length = jnp.dot(few, table((count, slots8), 1, False), preferred_element_type=F32)[:8]
    source = source_row((8, slots8), 1, start, length)[:1]
    hit = lax.broadcasted_iota(jnp.int32, (rows, slots8), 0) == source
    pick_ref[...] = jnp.where(hit, F32(1.0), F32(0.0)).astype(BF16)

    contract = (((1,), (1,)), ((), ()))
    start = lax.dot_general(table((slots8, count), 0, True), many, contract, preferred_element_type=F32)
    length = lax.dot_general(table((slots8, count), 0, False), many, contract, preferred_element_type=F32)
    source = source_row((slots8, LANES), 0, start, length)
    for at in range(0, rows, LANES):
        some = min(LANES, rows - at)
        hit = lax.broadcasted_iota(jnp.int32, (slots8, some), 1) + at == source[:, :some]
        place_ref[:, at:at + some] = jnp.where(hit, F32(1.0), F32(0.0)).astype(BF16)


def in_half(shape, half):
    return (lax.broadcasted_iota(jnp.int32, shape, 0) // 4) % 2 == half


def compact_kernel(pick_ref, in_ref, _, out_ref):
    slots8 = pick_ref.shape[1]
    upper = in_half((slots8, LANES), 0)
    got = in_ref[...].astype(F32)
    both = jnp.concatenate([jnp.where(upper, got, 0.0), jnp.where(upper, 0.0, got)], axis=1).astype(BF16)
    picked = jnp.dot(pick_ref[...], both, preferred_element_type=F32).astype(BF16)
    for rep in range(out_ref.shape[0]):
        out_ref[rep] = picked


def newton_schulz_kernel(scale, pieces_ref, scaled_ref, x, gram, poly):
    wide = 2 * LANES
    blocks, rows = pieces_ref.shape[:2]
    tiles = [slice(block * wide, (block + 1) * wide) for block in range(blocks)]
    fold = rows // 4
    low = rows * 2 // 3
    partial = jnp.zeros((fold, wide), F32)
    for at in range(0, rows, fold):
        squares = [pieces_ref[block, at:at + fold, :].astype(F32) for block in range(blocks)]
        squares = [piece * piece for piece in squares]
        partial = partial + ((squares[0] + squares[1]) + (squares[2] + squares[3]))
    factor = 1.0 / (jnp.sqrt(jnp.full((1, wide), jnp.sum(partial), F32)) + 1e-07)
    for block, tile in enumerate(tiles):
        x[:, tile] = (pieces_ref[block].astype(F32) * factor).astype(BF16)

    def poly_of():
        contract = (((1,), (1,)), ((), ()))
        for at, left in ((0, x[...]), (low, x[low:, :])):
            right = x[at:at + low, :]
            part = lax.dot_general(left, right, contract, preferred_element_type=F32)
            gram[at:, at:at + low] = part.astype(BF16)
            if at == 0:
                gram[:low, low:] = part[low:, :].T.astype(BF16)
        for at in (0, low):
            part = jnp.dot(gram[at:, :], gram[:, at:at + low], preferred_element_type=F32)
            part = COEF_B * gram[at:, at:at + low].astype(F32) + COEF_C * part
            poly[at:, at:at + low] = part.astype(BF16)
            if at == 0:
                poly[:low, low:] = part[low:, :].T.astype(BF16)
        return poly[...]

    def next_of(now, tile):
        part = x[:, tile]
        return (COEF_A * part.astype(F32) + jnp.dot(now, part, preferred_element_type=F32)).astype(BF16)

    def step(index, carry):
        now = poly_of()
        for tile in tiles:
            x[:, tile] = next_of(now, tile)
        return carry

    lax.fori_loop(0, ITERS - 1, step, 0)
    last = poly_of()
    for tile in tiles:
        scaled_ref[:, tile] = (-scale * next_of(last, tile).astype(F32)).astype(BF16)


def place_kernel(place_ref, scaled_ref, total_ref, first_ref, back_ref, joined_ref, back, sems):
    rows8 = total_ref.shape[0]
    mine = scaled_ref[:, pl.ds(column_of(0, lax.axis_index("rep")), 2 * LANES)]
    some = back_ref.shape[0] // 2
    upper = in_half((some, LANES), 0)
    copies = []
    for half in range(2):
        at = slice(half * some, (half + 1) * some)
        spread = jnp.dot(place_ref[at, :], mine, preferred_element_type=F32)
        back[at, :] = jnp.where(upper, spread[:, :LANES], spread[:, LANES:]).astype(BF16)
        copies.append(pltpu.make_async_copy(back.at[at], back_ref.at[at], sems.at[half]))
        copies[-1].start()
    joined_ref[:rows8, :] = total_ref[...]
    joined_ref[rows8:, :] = first_ref[...]
    for copy in copies:
        copy.wait()


def owned_kernel(scaled_ref, _, owned_ref, done_ref):
    owned_ref[...] = scaled_ref[...]
    done_ref[...] = jnp.zeros_like(done_ref)


def select_kernel(owner_ref, back_ref, _, out_ref, wide, chosen):
    wide[...] = back_ref[...].astype(F32)
    for m in range(chosen.shape[0] // ROWS):
        at = pl.multiple_of(owner_ref[m] * ROWS, ROWS)
        chosen[m * ROWS:(m + 1) * ROWS, :] = wide[pl.ds(at, ROWS), :]
    rounded = chosen[...].astype(BF16)
    for rep in range(out_ref.shape[0]):
        out_ref[rep] = rounded


def partners():
    core = lax.rem(lax.axis_index("fsdp"), 2)
    return 1 + 2 * core, 3 - 2 * core


def blocks_of(own_ref, first_ref, second_ref):
    me = lax.axis_index("rep")
    first, second = partners()
    rows = own_ref.shape[0]
    return (
        (me, own_ref),
        (me ^ first, first_ref),
        (me ^ second, second_ref.at[:rows]),
        (me ^ 2, second_ref.at[rows:]),
    )


def columns(blocks, count):
    slots = ROWS // 2
    for block, piece in blocks:
        got = piece[...].astype(F32).reshape(count, ROWS, LANES)
        for half in range(2):
            yield pl.ds(column_of(half, block), LANES), got[:, half * slots:(half + 1) * slots, :]


def update_kernel(pieces_ref, out_ref):
    for at, got in columns([(block, pieces_ref.at[block]) for block in range(pieces_ref.shape[0])], out_ref.shape[0]):
        out_ref[:, :, at] = got.astype(BF16)


def momentum_kernel(lens_ref, mom_ref, own_ref, first_ref, second_ref, _, out_ref, done_ref, total):
    done_ref[...] = jnp.zeros_like(done_ref)
    device = lax.axis_index("fsdp")
    count, slots, width = out_ref.shape
    for at, got in columns(blocks_of(own_ref, first_ref, second_ref), count):
        total[:, :, at] = got
    slot = lax.broadcasted_iota(jnp.int32, (slots, width), 0)
    for m in range(count):
        live = slot < lens_ref[m, device]
        out_ref[m] = jnp.where(live, 0.95 * mom_ref[m] + total[m], 0.0)


def swap(value, step):
    devices, reps = lax.axis_size("fsdp"), lax.axis_size("rep")
    pairs = []
    for device in range(devices):
        flip = (1, 3)[(device + step) % 2]
        pairs += [(device * reps + rep, device * reps + (rep ^ flip)) for rep in range(reps)]
    return lax.ppermute(value, ("fsdp", "rep"), pairs)


def exchange(value):
    flat = value.reshape((value.shape[0] * value.shape[1],) + value.shape[2:])
    return lax.all_to_all(flat, "rep", split_axis=0, concat_axis=0, tiled=True).reshape(value.shape)


def body(grads, momentum, lengths, owner):
    reps = lax.axis_size("rep")
    devices = lax.axis_size("fsdp")
    count, slots, width = momentum.shape[1:]
    g, mom = grads[0, 0], momentum[0]
    rows8, slots8 = count * ROWS, devices * ROWS
    shape = jax.ShapeDtypeStruct
    part = shape((rows8, LANES), BF16)
    parts = shape((reps, rows8, LANES), BF16)

    split = pl.pallas_call(
        split_kernel,
        out_shape=parts,
        in_specs=[hbm()],
        out_specs=hbm(),
        scratch_shapes=[
            pltpu.VMEM((reps, count, slots, 2 * LANES), F32),
            pltpu.VMEM((reps, count, ROWS, LANES), F32),
            pltpu.VMEM((reps, rows8, LANES), BF16),
            pltpu.SemaphoreType.DMA((reps,)),
            pltpu.SemaphoreType.DMA((reps,)),
        ],
        compiler_params=params(60 * 1024 * 1024),
        cost_estimate=cost(0, 2_000_000),
        name="split",
    )(g)
    got = exchange(split)
    base, pick, place = pl.pallas_call(
        own_kernel,
        out_shape=[shape((rows8, LANES), F32), shape((R, slots8), BF16), shape((slots8, R), BF16)],
        in_specs=[smem()] + [vmem()] * 2,
        out_specs=[vmem()] * 3,
        scratch_shapes=[pltpu.VMEM((count, ROWS, LANES), F32)],
        compiler_params=params(),
        cost_estimate=cost(0, 4_000_000),
        name="own",
    )(owner, lengths, mom)
    send, total = pl.pallas_call(
        scatter_kernel,
        out_shape=[shape((slots8, LANES), BF16), part],
        in_specs=[smem(), vmem(), vmem()],
        out_specs=[vmem()] * 2,
        scratch_shapes=[pltpu.VMEM((slots8, LANES), F32)],
        compiler_params=params(),
        cost_estimate=cost(0, 2_000_000),
        name="scatter",
    )(owner, base, got)
    first = swap(total, 0)
    incoming = lax.all_to_all(send, "fsdp", split_axis=0, concat_axis=0, tiled=True)
    compact = pl.pallas_call(
        compact_kernel,
        out_shape=shape((reps, R, 2 * LANES), BF16),
        in_specs=[vmem()] * 2 + [later()],
        out_specs=vmem(),
        compiler_params=params(),
        cost_estimate=cost(200_000_000, 2_000_000),
        name="compact",
    )(pick, incoming, first)

    pieces = exchange(compact)
    scaled = pl.pallas_call(
        functools.partial(newton_schulz_kernel, math.sqrt(max(R, width))),
        out_shape=shape((R, width), BF16),
        in_specs=[vmem()],
        out_specs=vmem(),
        scratch_shapes=[pltpu.VMEM((R, width), BF16), pltpu.VMEM((R, R), BF16), pltpu.VMEM((R, R), BF16)],
        compiler_params=params(),
        cost_estimate=cost(5_000_000_000, 4_000_000),
        name="newton_schulz",
    )(pieces)
    back, joined = pl.pallas_call(
        place_kernel,
        out_shape=[shape((slots8, LANES), BF16), shape((2 * rows8, LANES), BF16)],
        in_specs=[vmem()] * 4,
        out_specs=[hbm(), vmem()],
        scratch_shapes=[pltpu.VMEM((slots8, LANES), BF16), pltpu.SemaphoreType.DMA((2,))],
        compiler_params=params(),
        cost_estimate=cost(200_000_000, 2_000_000),
        name="place",
    )(place, scaled, total, first)
    owned, written = pl.pallas_call(
        owned_kernel,
        out_shape=[shape((R, width), BF16), shape((8, LANES), F32)],
        in_specs=[vmem(), later()],
        out_specs=[vmem()] * 2,
        compiler_params=params(),
        cost_estimate=cost(0, 2_000_000),
        name="owned",
    )(scaled, joined)
    returned = lax.all_to_all(back, "fsdp", split_axis=0, concat_axis=0, tiled=True)
    new_momentum, done = pl.pallas_call(
        momentum_kernel,
        out_shape=[shape((count, slots, width), F32), shape((8, LANES), F32)],
        in_specs=[smem()] + [vmem()] * 4 + [later()],
        out_specs=[vmem()] * 2,
        scratch_shapes=[pltpu.VMEM((count, slots, width), F32)],
        compiler_params=params(),
        cost_estimate=cost(0, 4_000_000),
        name="momentum",
    )(lengths, mom, total, first, swap(joined, 1), written)
    chosen = pl.pallas_call(
        select_kernel,
        out_shape=parts,
        in_specs=[smem(), vmem(), later()],
        out_specs=vmem(),
        scratch_shapes=[pltpu.VMEM((slots8, LANES), F32), pltpu.VMEM((rows8, LANES), F32)],
        compiler_params=params(),
        cost_estimate=cost(0, 1_000_000),
        name="select",
    )(owner, returned, done)
    update = pl.pallas_call(
        update_kernel,
        out_shape=shape((count, slots, width), BF16),
        in_specs=[vmem()],
        out_specs=vmem(),
        compiler_params=params(),
        cost_estimate=cost(0, 2_000_000),
        name="update",
    )(exchange(chosen))
    return (new_momentum[None], update[None], owned[None])


def solution(mesh):
    in_specs = (P("rep", "fsdp", None, None, None), P("fsdp", None, None, None), P(), P())
    out_specs = (P("fsdp", None, None, None), P("fsdp", None, None, None), P("fsdp", None, None))
    return jax.shard_map(body, mesh=mesh, in_specs=in_specs, out_specs=out_specs, check_vma=False)
```

```python
import functools
import math

import jax
import jax.numpy as jnp
from jax import lax
from jax.experimental import pallas as pl
from jax.experimental.pallas import tpu as pltpu
from jax.sharding import PartitionSpec as P

R = 384
ITERS = 5

COEF_A = 3.4445
COEF_B = -4.775
COEF_C = 2.0315

LANES = 128
ROWS = 8
BF16 = jnp.bfloat16
F32 = jnp.float32
VMEM_LIMIT = 24 * 1024 * 1024
SPLIT_LIMIT = 60 * 1024 * 1024


def vmem():
    return pl.BlockSpec(memory_space=pltpu.VMEM)


def hbm():
    return pl.BlockSpec(memory_space=pltpu.HBM)


def later():
    return pl.BlockSpec(memory_space=pl.ANY)


def smem():
    return pl.BlockSpec(memory_space=pltpu.SMEM)


def params(limit=VMEM_LIMIT):
    return pltpu.CompilerParams(vmem_limit_bytes=limit)


def cost(flops, nbytes):
    return pl.CostEstimate(flops=flops, bytes_accessed=nbytes, transcendentals=0)


def column_of(half, block):
    if isinstance(block, int):
        return block * 2 * LANES + half * LANES
    return pl.multiple_of(block * (2 * LANES) + half * LANES, LANES)


def to_rows(src_ref, block, scratch):
    slots = src_ref.shape[1]
    for half in range(2):
        scratch[:, half * slots:(half + 1) * slots, :] = src_ref[:, :, pl.ds(column_of(half, block), LANES)]
    return scratch[...].reshape(scratch.shape[0] * ROWS, LANES)


def split_kernel(g_ref, out_ref, arrived, scratch, packed, in_sems, out_sems):
    blocks = out_ref.shape[0]
    wide = 2 * LANES
    reads = [
        pltpu.make_async_copy(g_ref.at[:, :, block * wide:(block + 1) * wide], arrived.at[block], in_sems.at[block])
        for block in range(blocks)
    ]
    writes = [pltpu.make_async_copy(packed.at[block], out_ref.at[block], out_sems.at[block]) for block in range(blocks)]
    for read in reads:
        read.start()
    for block in range(blocks):
        reads[block].wait()
        packed[block] = to_rows(arrived.at[block], 0, scratch.at[block]).astype(BF16)
        writes[block].start()
    for write in writes:
        write.wait()


def own_kernel(owner_ref, lens_ref, mom_ref, base_ref, pick_ref, place_ref, scratch):
    base_ref[...] = 0.95 * to_rows(mom_ref, lax.axis_index("rep"), scratch)
    pick_kernel(owner_ref, lens_ref, pick_ref, place_ref)


def scatter_kernel(owner_ref, base_ref, parts_ref, send_ref, tot_ref, packed):
    reps = parts_ref.shape[0]
    total = parts_ref[0].astype(F32)
    for rep in range(1, reps):
        total = total + parts_ref[rep].astype(F32)
    tot_ref[...] = total.astype(BF16)
    nm = base_ref[...] + total
    packed[...] = jnp.zeros_like(packed)
    for m in range(nm.shape[0] // ROWS):
        at = pl.multiple_of(owner_ref[m] * ROWS, ROWS)
        packed[pl.ds(at, ROWS), :] = nm[m * ROWS:(m + 1) * ROWS, :]
    send_ref[...] = packed[...].astype(BF16)


def pick_kernel(owner_ref, lens_ref, pick_ref, place_ref):
    me = lax.axis_index("fsdp")
    rows, slots8 = pick_ref.shape
    count = lens_ref.shape[1]

    def find(m, found):
        return jnp.where(owner_ref[m] == me, m, found)

    mine = lax.fori_loop(0, lens_ref.shape[0], find, -1)
    lens = lens_ref[pl.ds(jnp.maximum(mine, 0), 1), :]
    lens = jnp.where(mine >= 0, lens, 0).astype(F32)
    many = jnp.broadcast_to(lens, (LANES, count)).astype(BF16)

    def table(shape, slot_dim, before):
        device = lax.broadcasted_iota(jnp.int32, shape, 1 - slot_dim)
        source = lax.broadcasted_iota(jnp.int32, shape, slot_dim) // ROWS
        hit = device < source if before else device == source
        return jnp.where(hit, F32(1.0), F32(0.0)).astype(BF16)

    def source_row(shape, slot_dim, start, length):
        slot = (lax.broadcasted_iota(jnp.int32, shape, slot_dim) % 4)
        return jnp.where(slot < length.astype(jnp.int32), start.astype(jnp.int32) + slot, -1)

    few = many[:16, :]
    start = jnp.dot(few, table((count, slots8), 1, True), preferred_element_type=F32)[:8]
    length = jnp.dot(few, table((count, slots8), 1, False), preferred_element_type=F32)[:8]
    source = source_row((8, slots8), 1, start, length)[:1]
    hit = lax.broadcasted_iota(jnp.int32, (rows, slots8), 0) == source
    pick_ref[...] = jnp.where(hit, F32(1.0), F32(0.0)).astype(BF16)

    contract = (((1,), (1,)), ((), ()))
    start = lax.dot_general(table((slots8, count), 0, True), many, contract, preferred_element_type=F32)
    length = lax.dot_general(table((slots8, count), 0, False), many, contract, preferred_element_type=F32)
    source = source_row((slots8, LANES), 0, start, length)
    for at in range(0, rows, LANES):
        some = min(LANES, rows - at)
        hit = lax.broadcasted_iota(jnp.int32, (slots8, some), 1) + at == source[:, :some]
        place_ref[:, at:at + some] = jnp.where(hit, F32(1.0), F32(0.0)).astype(BF16)


def in_half(shape, half):
    return (lax.broadcasted_iota(jnp.int32, shape, 0) // 4) % 2 == half


def compact_kernel(pick_ref, in_ref, _, out_ref):
    slots8 = pick_ref.shape[1]
    upper = in_half((slots8, LANES), 0)
    got = in_ref[...].astype(F32)
    both = jnp.concatenate([jnp.where(upper, got, 0.0), jnp.where(upper, 0.0, got)], axis=1).astype(BF16)
    picked = jnp.dot(pick_ref[...], both, preferred_element_type=F32).astype(BF16)
    for rep in range(out_ref.shape[0]):
        out_ref[rep] = picked


def newton_schulz_kernel(scale, place_ref, pieces_ref, total_ref, first_ref, scaled_ref, back_ref, joined_ref, x):
    rows8 = total_ref.shape[0]
    joined_ref[:rows8, :] = total_ref[...]
    joined_ref[rows8:, :] = first_ref[...]
    wide = 2 * LANES
    blocks, rows = pieces_ref.shape[:2]
    tiles = [slice(block * wide, (block + 1) * wide) for block in range(blocks)]
    fold = rows // 4
    partial = jnp.zeros((fold, wide), F32)
    for at in range(0, rows, fold):
        squares = [pieces_ref[block, at:at + fold, :].astype(F32) for block in range(blocks)]
        squares = [piece * piece for piece in squares]
        partial = partial + ((squares[0] + squares[1]) + (squares[2] + squares[3]))
    factor = 1.0 / (jnp.sqrt(jnp.full((1, wide), jnp.sum(partial), F32)) + 1e-07)
    for block, tile in enumerate(tiles):
        x[:, tile] = (pieces_ref[block].astype(F32) * factor).astype(BF16)

    def poly_of():
        contract = (((1,), (1,)), ((), ()))
        gram = lax.dot_general(x[...], x[...], contract, preferred_element_type=F32).astype(BF16)
        square = jnp.dot(gram, gram, preferred_element_type=F32)
        return (COEF_B * gram.astype(F32) + COEF_C * square).astype(BF16)

    def next_of(poly, tile):
        part = x[:, tile]
        return (COEF_A * part.astype(F32) + jnp.dot(poly, part, preferred_element_type=F32)).astype(BF16)

    def step(index, carry):
        poly = poly_of()
        for tile in tiles:
            x[:, tile] = next_of(poly, tile)
        return carry

    lax.fori_loop(0, ITERS - 1, step, 0)
    poly = poly_of()
    for tile in tiles:
        scaled_ref[:, tile] = (-scale * next_of(poly, tile).astype(F32)).astype(BF16)
    mine = scaled_ref[:, pl.ds(column_of(0, lax.axis_index("rep")), wide)]
    upper = in_half((place_ref.shape[0], LANES), 0)
    spread = jnp.dot(place_ref[...], mine, preferred_element_type=F32)
    back_ref[...] = jnp.where(upper, spread[:, :LANES], spread[:, LANES:]).astype(BF16)


def owned_kernel(scaled_ref, _, owned_ref, done_ref):
    owned_ref[...] = scaled_ref[...]
    done_ref[...] = jnp.zeros_like(done_ref)


def select_kernel(owner_ref, back_ref, _, out_ref, wide, chosen):
    wide[...] = back_ref[...].astype(F32)
    for m in range(chosen.shape[0] // ROWS):
        at = pl.multiple_of(owner_ref[m] * ROWS, ROWS)
        chosen[m * ROWS:(m + 1) * ROWS, :] = wide[pl.ds(at, ROWS), :]
    rounded = chosen[...].astype(BF16)
    for rep in range(out_ref.shape[0]):
        out_ref[rep] = rounded


def partners():
    core = lax.rem(lax.axis_index("fsdp"), 2)
    return 1 + 2 * core, 3 - 2 * core


def blocks_of(own_ref, first_ref, second_ref):
    me = lax.axis_index("rep")
    first, second = partners()
    rows = own_ref.shape[0]
    return (
        (me, own_ref),
        (me ^ first, first_ref),
        (me ^ second, second_ref.at[:rows]),
        (me ^ 2, second_ref.at[rows:]),
    )


def columns(blocks, count):
    slots = ROWS // 2
    for block, piece in blocks:
        got = piece[...].astype(F32).reshape(count, ROWS, LANES)
        for half in range(2):
            yield pl.ds(column_of(half, block), LANES), got[:, half * slots:(half + 1) * slots, :]


def update_kernel(pieces_ref, out_ref):
    for at, got in columns([(block, pieces_ref.at[block]) for block in range(pieces_ref.shape[0])], out_ref.shape[0]):
        out_ref[:, :, at] = got.astype(BF16)


def momentum_kernel(lens_ref, mom_ref, own_ref, first_ref, second_ref, _, out_ref, done_ref, total):
    done_ref[...] = jnp.zeros_like(done_ref)
    device = lax.axis_index("fsdp")
    count, slots, width = out_ref.shape
    for at, got in columns(blocks_of(own_ref, first_ref, second_ref), count):
        total[:, :, at] = got
    slot = lax.broadcasted_iota(jnp.int32, (slots, width), 0)
    for m in range(count):
        live = slot < lens_ref[m, device]
        out_ref[m] = jnp.where(live, 0.95 * mom_ref[m] + total[m], 0.0)


def swap(value, step):
    devices, reps = lax.axis_size("fsdp"), lax.axis_size("rep")
    pairs = []
    for device in range(devices):
        flip = (1, 3)[(device + step) % 2]
        pairs += [(device * reps + rep, device * reps + (rep ^ flip)) for rep in range(reps)]
    return lax.ppermute(value, ("fsdp", "rep"), pairs)


def exchange(value):
    flat = value.reshape((value.shape[0] * value.shape[1],) + value.shape[2:])
    return lax.all_to_all(flat, "rep", split_axis=0, concat_axis=0, tiled=True).reshape(value.shape)


def body(grads, momentum, lengths, owner):
    reps = lax.axis_size("rep")
    devices = lax.axis_size("fsdp")
    count, slots, width = momentum.shape[1:]
    g, mom = grads[0, 0], momentum[0]
    rows8, slots8 = count * ROWS, devices * ROWS
    shape = jax.ShapeDtypeStruct
    part = shape((rows8, LANES), BF16)
    parts = shape((reps, rows8, LANES), BF16)

    split = pl.pallas_call(
        split_kernel,
        out_shape=parts,
        in_specs=[hbm()],
        out_specs=hbm(),
        scratch_shapes=[
            pltpu.VMEM((reps, count, slots, 2 * LANES), F32),
            pltpu.VMEM((reps, count, ROWS, LANES), F32),
            pltpu.VMEM((reps, rows8, LANES), BF16),
            pltpu.SemaphoreType.DMA((reps,)),
            pltpu.SemaphoreType.DMA((reps,)),
        ],
        compiler_params=params(SPLIT_LIMIT),
        cost_estimate=cost(0, 2_000_000),
        name="split",
    )(g)
    got = exchange(split)
    base, pick, place = pl.pallas_call(
        own_kernel,
        out_shape=[shape((rows8, LANES), F32), shape((R, slots8), BF16), shape((slots8, R), BF16)],
        in_specs=[smem()] + [vmem()] * 2,
        out_specs=[vmem()] * 3,
        scratch_shapes=[pltpu.VMEM((count, ROWS, LANES), F32)],
        compiler_params=params(),
        cost_estimate=cost(0, 4_000_000),
        name="own",
    )(owner, lengths, mom)
    send, total = pl.pallas_call(
        scatter_kernel,
        out_shape=[shape((slots8, LANES), BF16), part],
        in_specs=[smem(), vmem(), vmem()],
        out_specs=[vmem()] * 2,
        scratch_shapes=[pltpu.VMEM((slots8, LANES), F32)],
        compiler_params=params(),
        cost_estimate=cost(0, 2_000_000),
        name="scatter",
    )(owner, base, got)
    first = swap(total, 0)
    incoming = lax.all_to_all(send, "fsdp", split_axis=0, concat_axis=0, tiled=True)
    compact = pl.pallas_call(
        compact_kernel,
        out_shape=shape((reps, R, 2 * LANES), BF16),
        in_specs=[vmem()] * 2 + [later()],
        out_specs=vmem(),
        compiler_params=params(),
        cost_estimate=cost(200_000_000, 2_000_000),
        name="compact",
    )(pick, incoming, first)

    pieces = exchange(compact)
    scaled, back, joined = pl.pallas_call(
        functools.partial(newton_schulz_kernel, math.sqrt(max(R, width))),
        out_shape=[shape((R, width), BF16), shape((slots8, LANES), BF16), shape((2 * rows8, LANES), BF16)],
        in_specs=[vmem()] * 4,
        out_specs=[vmem()] * 3,
        scratch_shapes=[pltpu.VMEM((R, width), BF16)],
        compiler_params=params(),
        cost_estimate=cost(5_000_000_000, 4_000_000),
        name="newton_schulz",
    )(place, pieces, total, first)
    owned, written = pl.pallas_call(
        owned_kernel,
        out_shape=[shape((R, width), BF16), shape((8, LANES), F32)],
        in_specs=[vmem(), later()],
        out_specs=[vmem()] * 2,
        compiler_params=params(),
        cost_estimate=cost(0, 2_000_000),
        name="owned",
    )(scaled, joined)
    returned = lax.all_to_all(back, "fsdp", split_axis=0, concat_axis=0, tiled=True)
    new_momentum, done = pl.pallas_call(
        momentum_kernel,
        out_shape=[shape((count, slots, width), F32), shape((8, LANES), F32)],
        in_specs=[smem()] + [vmem()] * 4 + [later()],
        out_specs=[vmem()] * 2,
        scratch_shapes=[pltpu.VMEM((count, slots, width), F32)],
        compiler_params=params(),
        cost_estimate=cost(0, 4_000_000),
        name="momentum",
    )(lengths, mom, total, first, swap(joined, 1), written)
    chosen = pl.pallas_call(
        select_kernel,
        out_shape=parts,
        in_specs=[smem(), vmem(), later()],
        out_specs=vmem(),
        scratch_shapes=[pltpu.VMEM((slots8, LANES), F32), pltpu.VMEM((rows8, LANES), F32)],
        compiler_params=params(),
        cost_estimate=cost(0, 1_000_000),
        name="select",
    )(owner, returned, done)
    update = pl.pallas_call(
        update_kernel,
        out_shape=shape((count, slots, width), BF16),
        in_specs=[vmem()],
        out_specs=vmem(),
        compiler_params=params(),
        cost_estimate=cost(0, 2_000_000),
        name="update",
    )(exchange(chosen))
    return (new_momentum[None], update[None], owned[None])


def solution(mesh):
    in_specs = (P("rep", "fsdp", None, None, None), P("fsdp", None, None, None), P(), P())
    out_specs = (P("fsdp", None, None, None), P("fsdp", None, None, None), P("fsdp", None, None))
    return jax.shard_map(body, mesh=mesh, in_specs=in_specs, out_specs=out_specs, check_vma=False)
```

```python
import functools
import math

import jax
import jax.numpy as jnp
from jax import lax
from jax.experimental import pallas as pl
from jax.experimental.pallas import tpu as pltpu
from jax.sharding import PartitionSpec as P

R = 384
ITERS = 5

COEF_A = 3.4445
COEF_B = -4.775
COEF_C = 2.0315

LANES = 128
ROWS = 8
UPDATE_PARTS = 3
BF16 = jnp.bfloat16
F32 = jnp.float32
VMEM_LIMIT = 24 * 1024 * 1024
SPLIT_LIMIT = 60 * 1024 * 1024


def vmem():
    return pl.BlockSpec(memory_space=pltpu.VMEM)


def hbm():
    return pl.BlockSpec(memory_space=pltpu.HBM)


def later():
    return pl.BlockSpec(memory_space=pl.ANY)


def smem():
    return pl.BlockSpec(memory_space=pltpu.SMEM)


def params(limit=VMEM_LIMIT):
    return pltpu.CompilerParams(vmem_limit_bytes=limit)


def cost(flops, nbytes):
    return pl.CostEstimate(flops=flops, bytes_accessed=nbytes, transcendentals=0)


def column_of(half, block):
    if isinstance(block, int):
        return block * 2 * LANES + half * LANES
    return pl.multiple_of(block * (2 * LANES) + half * LANES, LANES)


def to_rows(src_ref, block, scratch):
    slots = src_ref.shape[1]
    for half in range(2):
        scratch[:, half * slots:(half + 1) * slots, :] = src_ref[:, :, pl.ds(column_of(half, block), LANES)]
    return scratch[...].reshape(scratch.shape[0] * ROWS, LANES)


def split_kernel(g_ref, out_ref, arrived, scratch, packed, in_sems, out_sems):
    blocks = out_ref.shape[0]
    wide = 2 * LANES
    reads = [
        pltpu.make_async_copy(g_ref.at[:, :, block * wide:(block + 1) * wide], arrived.at[block], in_sems.at[block])
        for block in range(blocks)
    ]
    writes = [pltpu.make_async_copy(packed.at[block], out_ref.at[block], out_sems.at[block]) for block in range(blocks)]
    for read in reads:
        read.start()
    for block in range(blocks):
        reads[block].wait()
        packed[block] = to_rows(arrived.at[block], 0, scratch.at[block]).astype(BF16)
        writes[block].start()
    for write in writes:
        write.wait()


def own_kernel(owner_ref, lens_ref, mom_ref, base_ref, pick_ref, place_ref, scratch):
    base_ref[...] = 0.95 * to_rows(mom_ref, lax.axis_index("rep"), scratch)
    pick_kernel(owner_ref, lens_ref, pick_ref, place_ref)


def scatter_kernel(owner_ref, base_ref, parts_ref, send_ref, tot_ref, packed):
    reps = parts_ref.shape[0]
    total = parts_ref[0].astype(F32)
    for rep in range(1, reps):
        total = total + parts_ref[rep].astype(F32)
    tot_ref[...] = total.astype(BF16)
    nm = base_ref[...] + total
    packed[...] = jnp.zeros_like(packed)
    for m in range(nm.shape[0] // ROWS):
        at = pl.multiple_of(owner_ref[m] * ROWS, ROWS)
        packed[pl.ds(at, ROWS), :] = nm[m * ROWS:(m + 1) * ROWS, :]
    send_ref[...] = packed[...].astype(BF16)


def pick_kernel(owner_ref, lens_ref, pick_ref, place_ref):
    me = lax.axis_index("fsdp")
    rows, slots8 = pick_ref.shape
    count = lens_ref.shape[1]

    def find(m, found):
        return jnp.where(owner_ref[m] == me, m, found)

    mine = lax.fori_loop(0, lens_ref.shape[0], find, -1)
    lens = lens_ref[pl.ds(jnp.maximum(mine, 0), 1), :]
    lens = jnp.where(mine >= 0, lens, 0).astype(F32)
    many = jnp.broadcast_to(lens, (LANES, count)).astype(BF16)

    def table(shape, slot_dim, before):
        device = lax.broadcasted_iota(jnp.int32, shape, 1 - slot_dim)
        source = lax.broadcasted_iota(jnp.int32, shape, slot_dim) // ROWS
        hit = device < source if before else device == source
        return jnp.where(hit, F32(1.0), F32(0.0)).astype(BF16)

    def source_row(shape, slot_dim, start, length):
        slot = (lax.broadcasted_iota(jnp.int32, shape, slot_dim) % 4)
        return jnp.where(slot < length.astype(jnp.int32), start.astype(jnp.int32) + slot, -1)

    few = many[:16, :]
    start = jnp.dot(few, table((count, slots8), 1, True), preferred_element_type=F32)[:8]
    length = jnp.dot(few, table((count, slots8), 1, False), preferred_element_type=F32)[:8]
    source = source_row((8, slots8), 1, start, length)[:1]
    hit = lax.broadcasted_iota(jnp.int32, (rows, slots8), 0) == source
    pick_ref[...] = jnp.where(hit, F32(1.0), F32(0.0)).astype(BF16)

    contract = (((1,), (1,)), ((), ()))
    start = lax.dot_general(table((slots8, count), 0, True), many, contract, preferred_element_type=F32)
    length = lax.dot_general(table((slots8, count), 0, False), many, contract, preferred_element_type=F32)
    source = source_row((slots8, LANES), 0, start, length)
    for at in range(0, rows, LANES):
        some = min(LANES, rows - at)
        hit = lax.broadcasted_iota(jnp.int32, (slots8, some), 1) + at == source[:, :some]
        place_ref[:, at:at + some] = jnp.where(hit, F32(1.0), F32(0.0)).astype(BF16)


def in_half(shape, half):
    return (lax.broadcasted_iota(jnp.int32, shape, 0) // 4) % 2 == half


def compact_kernel(pick_ref, in_ref, _, out_ref):
    slots8 = pick_ref.shape[1]
    upper = in_half((slots8, LANES), 0)
    got = in_ref[...].astype(F32)
    both = jnp.concatenate([jnp.where(upper, got, 0.0), jnp.where(upper, 0.0, got)], axis=1).astype(BF16)
    picked = jnp.dot(pick_ref[...], both, preferred_element_type=F32).astype(BF16)
    for rep in range(out_ref.shape[0]):
        out_ref[rep] = picked


def newton_schulz_kernel(scale, place_ref, pieces_ref, total_ref, first_ref, scaled_ref, back_ref, joined_ref, x):
    rows8 = total_ref.shape[0]
    joined_ref[:rows8, :] = total_ref[...]
    joined_ref[rows8:, :] = first_ref[...]
    wide = 2 * LANES
    blocks, rows = pieces_ref.shape[:2]
    tiles = [slice(block * wide, (block + 1) * wide) for block in range(blocks)]
    fold = rows // 4
    partial = jnp.zeros((fold, wide), F32)
    for at in range(0, rows, fold):
        squares = [pieces_ref[block, at:at + fold, :].astype(F32) for block in range(blocks)]
        squares = [piece * piece for piece in squares]
        partial = partial + ((squares[0] + squares[1]) + (squares[2] + squares[3]))
    factor = 1.0 / (jnp.sqrt(jnp.full((1, wide), jnp.sum(partial), F32)) + 1e-07)
    for block, tile in enumerate(tiles):
        x[:, tile] = (pieces_ref[block].astype(F32) * factor).astype(BF16)

    def poly_of():
        contract = (((1,), (1,)), ((), ()))
        gram = lax.dot_general(x[...], x[...], contract, preferred_element_type=F32).astype(BF16)
        square = jnp.dot(gram, gram, preferred_element_type=F32)
        return (COEF_B * gram.astype(F32) + COEF_C * square).astype(BF16)

    pairs = [slice(at, at + 2 * wide) for at in range(0, blocks * wide, 2 * wide)]

    def next_of(poly, tile):
        part = x[:, tile]
        return (COEF_A * part.astype(F32) + jnp.dot(poly, part, preferred_element_type=F32)).astype(BF16)

    def step(index, carry):
        poly = poly_of()
        for tile in pairs:
            x[:, tile] = next_of(poly, tile)
        return carry

    lax.fori_loop(0, ITERS - 1, step, 0)
    poly = poly_of()
    for tile in pairs:
        scaled_ref[:, tile] = (-scale * next_of(poly, tile).astype(F32)).astype(BF16)
    mine = scaled_ref[:, pl.ds(column_of(0, lax.axis_index("rep")), wide)]
    upper = in_half((place_ref.shape[0], LANES), 0)
    spread = jnp.dot(place_ref[...], mine, preferred_element_type=F32)
    back_ref[...] = jnp.where(upper, spread[:, :LANES], spread[:, LANES:]).astype(BF16)


def owned_kernel(scaled_ref, _, owned_ref, done_ref):
    owned_ref[...] = scaled_ref[...]
    done_ref[...] = jnp.zeros_like(done_ref)


def select_kernel(owner_ref, back_ref, _, out_ref, wide, chosen):
    wide[...] = back_ref[...].astype(F32)
    for m in range(chosen.shape[0] // ROWS):
        at = pl.multiple_of(owner_ref[m] * ROWS, ROWS)
        chosen[m * ROWS:(m + 1) * ROWS, :] = wide[pl.ds(at, ROWS), :]
    rounded = chosen[...].astype(BF16)
    for rep in range(out_ref.shape[0]):
        out_ref[rep] = rounded


def partners():
    core = lax.rem(lax.axis_index("fsdp"), 2)
    return 1 + 2 * core, 3 - 2 * core


def blocks_of(own_ref, first_ref, second_ref):
    me = lax.axis_index("rep")
    first, second = partners()
    rows = own_ref.shape[0]
    return (
        (me, own_ref),
        (me ^ first, first_ref),
        (me ^ second, second_ref.at[:rows]),
        (me ^ 2, second_ref.at[rows:]),
    )


def columns(blocks, count):
    slots = ROWS // 2
    for block, piece in blocks:
        got = piece[...].astype(F32).reshape(count, ROWS, LANES)
        for half in range(2):
            yield pl.ds(column_of(half, block), LANES), got[:, half * slots:(half + 1) * slots, :]


def update_kernel(pieces_ref, out_ref, made, sems):
    count = made.shape[0]
    some = count // UPDATE_PARTS
    copies = []
    for at in range(0, count, some):
        blocks = [
            (block, pieces_ref.at[block, at * ROWS:(at + some) * ROWS, :]) for block in range(pieces_ref.shape[0])
        ]
        for lanes, got in columns(blocks, some):
            made[at:at + some, :, lanes] = got.astype(BF16)
        copies.append(pltpu.make_async_copy(made.at[at:at + some], out_ref.at[at:at + some], sems.at[len(copies)]))
        copies[-1].start()
    for copy in copies:
        copy.wait()


def momentum_kernel(lens_ref, mom_ref, own_ref, first_ref, second_ref, _, out_ref, done_ref, total):
    done_ref[...] = jnp.zeros_like(done_ref)
    device = lax.axis_index("fsdp")
    count, slots, width = out_ref.shape
    for at, got in columns(blocks_of(own_ref, first_ref, second_ref), count):
        total[:, :, at] = got
    slot = lax.broadcasted_iota(jnp.int32, (slots, width), 0)
    for m in range(count):
        live = slot < lens_ref[m, device]
        out_ref[m] = jnp.where(live, 0.95 * mom_ref[m] + total[m], 0.0)


def swap(value, step):
    devices, reps = lax.axis_size("fsdp"), lax.axis_size("rep")
    pairs = []
    for device in range(devices):
        flip = (1, 3)[(device + step) % 2]
        pairs += [(device * reps + rep, device * reps + (rep ^ flip)) for rep in range(reps)]
    return lax.ppermute(value, ("fsdp", "rep"), pairs)


def exchange(value):
    flat = value.reshape((value.shape[0] * value.shape[1],) + value.shape[2:])
    return lax.all_to_all(flat, "rep", split_axis=0, concat_axis=0, tiled=True).reshape(value.shape)


def body(grads, momentum, lengths, owner):
    reps = lax.axis_size("rep")
    devices = lax.axis_size("fsdp")
    count, slots, width = momentum.shape[1:]
    g, mom = grads[0, 0], momentum[0]
    rows8, slots8 = count * ROWS, devices * ROWS
    shape = jax.ShapeDtypeStruct
    part = shape((rows8, LANES), BF16)
    parts = shape((reps, rows8, LANES), BF16)

    split = pl.pallas_call(
        split_kernel,
        out_shape=parts,
        in_specs=[hbm()],
        out_specs=hbm(),
        scratch_shapes=[
            pltpu.VMEM((reps, count, slots, 2 * LANES), F32),
            pltpu.VMEM((reps, count, ROWS, LANES), F32),
            pltpu.VMEM((reps, rows8, LANES), BF16),
            pltpu.SemaphoreType.DMA((reps,)),
            pltpu.SemaphoreType.DMA((reps,)),
        ],
        compiler_params=params(SPLIT_LIMIT),
        cost_estimate=cost(0, 2_000_000),
        name="split",
    )(g)
    got = exchange(split)
    base, pick, place = pl.pallas_call(
        own_kernel,
        out_shape=[shape((rows8, LANES), F32), shape((R, slots8), BF16), shape((slots8, R), BF16)],
        in_specs=[smem()] + [vmem()] * 2,
        out_specs=[vmem()] * 3,
        scratch_shapes=[pltpu.VMEM((count, ROWS, LANES), F32)],
        compiler_params=params(),
        cost_estimate=cost(0, 4_000_000),
        name="own",
    )(owner, lengths, mom)
    send, total = pl.pallas_call(
        scatter_kernel,
        out_shape=[shape((slots8, LANES), BF16), part],
        in_specs=[smem(), vmem(), vmem()],
        out_specs=[vmem()] * 2,
        scratch_shapes=[pltpu.VMEM((slots8, LANES), F32)],
        compiler_params=params(),
        cost_estimate=cost(0, 2_000_000),
        name="scatter",
    )(owner, base, got)
    first = swap(total, 0)
    incoming = lax.all_to_all(send, "fsdp", split_axis=0, concat_axis=0, tiled=True)
    compact = pl.pallas_call(
        compact_kernel,
        out_shape=shape((reps, R, 2 * LANES), BF16),
        in_specs=[vmem()] * 2 + [later()],
        out_specs=vmem(),
        compiler_params=params(),
        cost_estimate=cost(200_000_000, 2_000_000),
        name="compact",
    )(pick, incoming, first)

    pieces = exchange(compact)
    scaled, back, joined = pl.pallas_call(
        functools.partial(newton_schulz_kernel, math.sqrt(max(R, width))),
        out_shape=[shape((R, width), BF16), shape((slots8, LANES), BF16), shape((2 * rows8, LANES), BF16)],
        in_specs=[vmem()] * 4,
        out_specs=[vmem()] * 3,
        scratch_shapes=[pltpu.VMEM((R, width), BF16)],
        compiler_params=params(),
        cost_estimate=cost(5_000_000_000, 4_000_000),
        name="newton_schulz",
    )(place, pieces, total, first)
    owned, written = pl.pallas_call(
        owned_kernel,
        out_shape=[shape((R, width), BF16), shape((8, LANES), F32)],
        in_specs=[vmem(), later()],
        out_specs=[vmem()] * 2,
        compiler_params=params(),
        cost_estimate=cost(0, 2_000_000),
        name="owned",
    )(scaled, joined)
    returned = lax.all_to_all(back, "fsdp", split_axis=0, concat_axis=0, tiled=True)
    new_momentum, done = pl.pallas_call(
        momentum_kernel,
        out_shape=[shape((count, slots, width), F32), shape((8, LANES), F32)],
        in_specs=[smem()] + [vmem()] * 4 + [later()],
        out_specs=[vmem()] * 2,
        scratch_shapes=[pltpu.VMEM((count, slots, width), F32)],
        compiler_params=params(),
        cost_estimate=cost(0, 4_000_000),
        name="momentum",
    )(lengths, mom, total, first, swap(joined, 1), written)
    chosen = pl.pallas_call(
        select_kernel,
        out_shape=parts,
        in_specs=[smem(), vmem(), later()],
        out_specs=vmem(),
        scratch_shapes=[pltpu.VMEM((slots8, LANES), F32), pltpu.VMEM((rows8, LANES), F32)],
        compiler_params=params(),
        cost_estimate=cost(0, 1_000_000),
        name="select",
    )(owner, returned, done)
    update = pl.pallas_call(
        update_kernel,
        out_shape=shape((count, slots, width), BF16),
        in_specs=[vmem()],
        out_specs=hbm(),
        scratch_shapes=[pltpu.VMEM((count, slots, width), BF16), pltpu.SemaphoreType.DMA((UPDATE_PARTS,))],
        compiler_params=params(),
        cost_estimate=cost(0, 2_000_000),
        name="update",
    )(exchange(chosen))
    return (new_momentum[None], update[None], owned[None])


def solution(mesh):
    in_specs = (P("rep", "fsdp", None, None, None), P("fsdp", None, None, None), P(), P())
    out_specs = (P("fsdp", None, None, None), P("fsdp", None, None, None), P("fsdp", None, None))
    return jax.shard_map(body, mesh=mesh, in_specs=in_specs, out_specs=out_specs, check_vma=False)
```

```python
import functools
import math

import jax
import jax.numpy as jnp
from jax import lax
from jax.experimental import pallas as pl
from jax.experimental.pallas import tpu as pltpu
from jax.sharding import PartitionSpec as P

R = 384
ITERS = 5

COEF_A = 3.4445
COEF_B = -4.775
COEF_C = 2.0315

LANES = 128
ROWS = 8
UPDATE_PARTS = 3
BF16 = jnp.bfloat16
F32 = jnp.float32
VMEM_LIMIT = 24 * 1024 * 1024
SPLIT_LIMIT = 60 * 1024 * 1024


def vmem():
    return pl.BlockSpec(memory_space=pltpu.VMEM)


def hbm():
    return pl.BlockSpec(memory_space=pltpu.HBM)


def later():
    return pl.BlockSpec(memory_space=pl.ANY)


def smem():
    return pl.BlockSpec(memory_space=pltpu.SMEM)


def params(limit=VMEM_LIMIT):
    return pltpu.CompilerParams(vmem_limit_bytes=limit)


def cost(flops, nbytes):
    return pl.CostEstimate(flops=flops, bytes_accessed=nbytes, transcendentals=0)


def column_of(half, block):
    if isinstance(block, int):
        return block * 2 * LANES + half * LANES
    return pl.multiple_of(block * (2 * LANES) + half * LANES, LANES)


def to_rows(src_ref, block, scratch):
    slots = src_ref.shape[1]
    for half in range(2):
        scratch[:, half * slots:(half + 1) * slots, :] = src_ref[:, :, pl.ds(column_of(half, block), LANES)]
    return scratch[...].reshape(scratch.shape[0] * ROWS, LANES)


def write_out(rows_of, made, out_ref, sems):
    parts = sems.shape[0]
    some = made.shape[0] // parts
    copies = []
    for part in range(parts):
        at = slice(part * some, (part + 1) * some)
        made[at, :] = rows_of(at)
        copies.append(pltpu.make_async_copy(made.at[at], out_ref.at[at], sems.at[part]))
        copies[-1].start()
    for copy in copies:
        copy.wait()


def split_kernel(g_ref, out_ref, arrived, scratch, packed, in_sems, out_sems):
    blocks = out_ref.shape[0]
    wide = 2 * LANES
    reads = [
        pltpu.make_async_copy(g_ref.at[:, :, block * wide:(block + 1) * wide], arrived.at[block], in_sems.at[block])
        for block in range(blocks)
    ]
    writes = [pltpu.make_async_copy(packed.at[block], out_ref.at[block], out_sems.at[block]) for block in range(blocks)]
    for read in reads:
        read.start()
    for block in range(blocks):
        reads[block].wait()
        packed[block] = to_rows(arrived.at[block], 0, scratch.at[block]).astype(BF16)
        writes[block].start()
    for write in writes:
        write.wait()


def own_kernel(owner_ref, lens_ref, mom_ref, base_ref, pick_ref, place_ref, scratch):
    base_ref[...] = 0.95 * to_rows(mom_ref, lax.axis_index("rep"), scratch)
    pick_kernel(owner_ref, lens_ref, pick_ref, place_ref)


def scatter_kernel(owner_ref, base_ref, parts_ref, send_ref, tot_ref, packed, rounded, sems):
    reps = parts_ref.shape[0]
    total = parts_ref[0].astype(F32)
    for rep in range(1, reps):
        total = total + parts_ref[rep].astype(F32)
    tot_ref[...] = total.astype(BF16)
    nm = base_ref[...] + total
    packed[...] = jnp.zeros_like(packed)
    for m in range(nm.shape[0] // ROWS):
        at = pl.multiple_of(owner_ref[m] * ROWS, ROWS)
        packed[pl.ds(at, ROWS), :] = nm[m * ROWS:(m + 1) * ROWS, :]
    write_out(lambda at: packed[at, :].astype(BF16), rounded, send_ref, sems)


def pick_kernel(owner_ref, lens_ref, pick_ref, place_ref):
    me = lax.axis_index("fsdp")
    rows, slots8 = pick_ref.shape
    count = lens_ref.shape[1]

    def find(m, found):
        return jnp.where(owner_ref[m] == me, m, found)

    mine = lax.fori_loop(0, lens_ref.shape[0], find, -1)
    lens = lens_ref[pl.ds(jnp.maximum(mine, 0), 1), :]
    lens = jnp.where(mine >= 0, lens, 0).astype(F32)
    many = jnp.broadcast_to(lens, (LANES, count)).astype(BF16)

    def table(shape, slot_dim, before):
        device = lax.broadcasted_iota(jnp.int32, shape, 1 - slot_dim)
        source = lax.broadcasted_iota(jnp.int32, shape, slot_dim) // ROWS
        hit = device < source if before else device == source
        return jnp.where(hit, F32(1.0), F32(0.0)).astype(BF16)

    def source_row(shape, slot_dim, start, length):
        slot = (lax.broadcasted_iota(jnp.int32, shape, slot_dim) % 4)
        return jnp.where(slot < length.astype(jnp.int32), start.astype(jnp.int32) + slot, -1)

    few = many[:16, :]
    start = jnp.dot(few, table((count, slots8), 1, True), preferred_element_type=F32)[:8]
    length = jnp.dot(few, table((count, slots8), 1, False), preferred_element_type=F32)[:8]
    source = source_row((8, slots8), 1, start, length)[:1]
    hit = lax.broadcasted_iota(jnp.int32, (rows, slots8), 0) == source
    pick_ref[...] = jnp.where(hit, F32(1.0), F32(0.0)).astype(BF16)

    contract = (((1,), (1,)), ((), ()))
    start = lax.dot_general(table((slots8, count), 0, True), many, contract, preferred_element_type=F32)
    length = lax.dot_general(table((slots8, count), 0, False), many, contract, preferred_element_type=F32)
    source = source_row((slots8, LANES), 0, start, length)
    for at in range(0, rows, LANES):
        some = min(LANES, rows - at)
        hit = lax.broadcasted_iota(jnp.int32, (slots8, some), 1) + at == source[:, :some]
        place_ref[:, at:at + some] = jnp.where(hit, F32(1.0), F32(0.0)).astype(BF16)


def in_half(shape, half):
    return (lax.broadcasted_iota(jnp.int32, shape, 0) // 4) % 2 == half


def compact_kernel(pick_ref, in_ref, _, out_ref):
    slots8 = pick_ref.shape[1]
    upper = in_half((slots8, LANES), 0)
    got = in_ref[...].astype(F32)
    both = jnp.concatenate([jnp.where(upper, got, 0.0), jnp.where(upper, 0.0, got)], axis=1).astype(BF16)
    picked = jnp.dot(pick_ref[...], both, preferred_element_type=F32).astype(BF16)
    for rep in range(out_ref.shape[0]):
        out_ref[rep] = picked


def newton_schulz_kernel(scale, place_ref, pieces_ref, total_ref, first_ref, scaled_ref, back_ref, joined_ref, x, made, sems):
    rows8 = total_ref.shape[0]
    joined_ref[:rows8, :] = total_ref[...]
    joined_ref[rows8:, :] = first_ref[...]
    wide = 2 * LANES
    blocks, rows = pieces_ref.shape[:2]
    tiles = [slice(block * wide, (block + 1) * wide) for block in range(blocks)]
    fold = rows // 4
    partial = jnp.zeros((fold, wide), F32)
    for at in range(0, rows, fold):
        squares = [pieces_ref[block, at:at + fold, :].astype(F32) for block in range(blocks)]
        squares = [piece * piece for piece in squares]
        partial = partial + ((squares[0] + squares[1]) + (squares[2] + squares[3]))
    factor = 1.0 / (jnp.sqrt(jnp.full((1, wide), jnp.sum(partial), F32)) + 1e-07)
    for block, tile in enumerate(tiles):
        x[:, tile] = (pieces_ref[block].astype(F32) * factor).astype(BF16)

    def poly_of():
        contract = (((1,), (1,)), ((), ()))
        gram = lax.dot_general(x[...], x[...], contract, preferred_element_type=F32).astype(BF16)
        square = jnp.dot(gram, gram, preferred_element_type=F32)
        return (COEF_B * gram.astype(F32) + COEF_C * square).astype(BF16)

    pairs = [slice(at, at + 2 * wide) for at in range(0, blocks * wide, 2 * wide)]

    def next_of(poly, tile):
        part = x[:, tile]
        return (COEF_A * part.astype(F32) + jnp.dot(poly, part, preferred_element_type=F32)).astype(BF16)

    def step(index, carry):
        poly = poly_of()
        for tile in pairs:
            x[:, tile] = next_of(poly, tile)
        return carry

    lax.fori_loop(0, ITERS - 1, step, 0)
    poly = poly_of()
    for tile in pairs:
        scaled_ref[:, tile] = (-scale * next_of(poly, tile).astype(F32)).astype(BF16)
    mine = scaled_ref[:, pl.ds(column_of(0, lax.axis_index("rep")), wide)]
    upper = in_half((place_ref.shape[0] // sems.shape[0], LANES), 0)

    def rows_of(at):
        spread = jnp.dot(place_ref[at, :], mine, preferred_element_type=F32)
        return jnp.where(upper, spread[:, :LANES], spread[:, LANES:]).astype(BF16)

    write_out(rows_of, made, back_ref, sems)


def owned_kernel(scaled_ref, _, owned_ref, done_ref):
    owned_ref[...] = scaled_ref[...]
    done_ref[...] = jnp.zeros_like(done_ref)


def select_kernel(owner_ref, back_ref, _, out_ref, wide, chosen):
    wide[...] = back_ref[...].astype(F32)
    for m in range(chosen.shape[0] // ROWS):
        at = pl.multiple_of(owner_ref[m] * ROWS, ROWS)
        chosen[m * ROWS:(m + 1) * ROWS, :] = wide[pl.ds(at, ROWS), :]
    rounded = chosen[...].astype(BF16)
    for rep in range(out_ref.shape[0]):
        out_ref[rep] = rounded


def partners():
    core = lax.rem(lax.axis_index("fsdp"), 2)
    return 1 + 2 * core, 3 - 2 * core


def blocks_of(own_ref, first_ref, second_ref):
    me = lax.axis_index("rep")
    first, second = partners()
    rows = own_ref.shape[0]
    return (
        (me, own_ref),
        (me ^ first, first_ref),
        (me ^ second, second_ref.at[:rows]),
        (me ^ 2, second_ref.at[rows:]),
    )


def columns(blocks, count):
    slots = ROWS // 2
    for block, piece in blocks:
        got = piece[...].astype(F32).reshape(count, ROWS, LANES)
        for half in range(2):
            yield pl.ds(column_of(half, block), LANES), got[:, half * slots:(half + 1) * slots, :]


def update_kernel(pieces_ref, out_ref, made, sems):
    count = made.shape[0]
    some = count // UPDATE_PARTS
    copies = []
    for at in range(0, count, some):
        blocks = [
            (block, pieces_ref.at[block, at * ROWS:(at + some) * ROWS, :]) for block in range(pieces_ref.shape[0])
        ]
        for lanes, got in columns(blocks, some):
            made[at:at + some, :, lanes] = got.astype(BF16)
        copies.append(pltpu.make_async_copy(made.at[at:at + some], out_ref.at[at:at + some], sems.at[len(copies)]))
        copies[-1].start()
    for copy in copies:
        copy.wait()


def momentum_kernel(lens_ref, mom_ref, own_ref, first_ref, second_ref, _, out_ref, done_ref, total):
    done_ref[...] = jnp.zeros_like(done_ref)
    device = lax.axis_index("fsdp")
    count, slots, width = out_ref.shape
    for at, got in columns(blocks_of(own_ref, first_ref, second_ref), count):
        total[:, :, at] = got
    slot = lax.broadcasted_iota(jnp.int32, (slots, width), 0)
    for m in range(count):
        live = slot < lens_ref[m, device]
        out_ref[m] = jnp.where(live, 0.95 * mom_ref[m] + total[m], 0.0)


def swap(value, step):
    devices, reps = lax.axis_size("fsdp"), lax.axis_size("rep")
    pairs = []
    for device in range(devices):
        flip = (1, 3)[(device + step) % 2]
        pairs += [(device * reps + rep, device * reps + (rep ^ flip)) for rep in range(reps)]
    return lax.ppermute(value, ("fsdp", "rep"), pairs)


def exchange(value):
    flat = value.reshape((value.shape[0] * value.shape[1],) + value.shape[2:])
    return lax.all_to_all(flat, "rep", split_axis=0, concat_axis=0, tiled=True).reshape(value.shape)


def body(grads, momentum, lengths, owner):
    reps = lax.axis_size("rep")
    devices = lax.axis_size("fsdp")
    count, slots, width = momentum.shape[1:]
    g, mom = grads[0, 0], momentum[0]
    rows8, slots8 = count * ROWS, devices * ROWS
    shape = jax.ShapeDtypeStruct
    part = shape((rows8, LANES), BF16)
    parts = shape((reps, rows8, LANES), BF16)

    split = pl.pallas_call(
        split_kernel,
        out_shape=parts,
        in_specs=[hbm()],
        out_specs=hbm(),
        scratch_shapes=[
            pltpu.VMEM((reps, count, slots, 2 * LANES), F32),
            pltpu.VMEM((reps, count, ROWS, LANES), F32),
            pltpu.VMEM((reps, rows8, LANES), BF16),
            pltpu.SemaphoreType.DMA((reps,)),
            pltpu.SemaphoreType.DMA((reps,)),
        ],
        compiler_params=params(SPLIT_LIMIT),
        cost_estimate=cost(0, 2_000_000),
        name="split",
    )(g)
    got = exchange(split)
    base, pick, place = pl.pallas_call(
        own_kernel,
        out_shape=[shape((rows8, LANES), F32), shape((R, slots8), BF16), shape((slots8, R), BF16)],
        in_specs=[smem()] + [vmem()] * 2,
        out_specs=[vmem()] * 3,
        scratch_shapes=[pltpu.VMEM((count, ROWS, LANES), F32)],
        compiler_params=params(),
        cost_estimate=cost(0, 4_000_000),
        name="own",
    )(owner, lengths, mom)
    send, total = pl.pallas_call(
        scatter_kernel,
        out_shape=[shape((slots8, LANES), BF16), part],
        in_specs=[smem(), vmem(), vmem()],
        out_specs=[hbm(), vmem()],
        scratch_shapes=[
            pltpu.VMEM((slots8, LANES), F32),
            pltpu.VMEM((slots8, LANES), BF16),
            pltpu.SemaphoreType.DMA((4,)),
        ],
        compiler_params=params(),
        cost_estimate=cost(0, 2_000_000),
        name="scatter",
    )(owner, base, got)
    first = swap(total, 0)
    incoming = lax.all_to_all(send, "fsdp", split_axis=0, concat_axis=0, tiled=True)
    compact = pl.pallas_call(
        compact_kernel,
        out_shape=shape((reps, R, 2 * LANES), BF16),
        in_specs=[vmem()] * 2 + [later()],
        out_specs=vmem(),
        compiler_params=params(),
        cost_estimate=cost(200_000_000, 2_000_000),
        name="compact",
    )(pick, incoming, first)

    pieces = exchange(compact)
    scaled, back, joined = pl.pallas_call(
        functools.partial(newton_schulz_kernel, math.sqrt(max(R, width))),
        out_shape=[shape((R, width), BF16), shape((slots8, LANES), BF16), shape((2 * rows8, LANES), BF16)],
        in_specs=[vmem()] * 4,
        out_specs=[vmem(), hbm(), vmem()],
        scratch_shapes=[
            pltpu.VMEM((R, width), BF16),
            pltpu.VMEM((slots8, LANES), BF16),
            pltpu.SemaphoreType.DMA((4,)),
        ],
        compiler_params=params(),
        cost_estimate=cost(5_000_000_000, 4_000_000),
        name="newton_schulz",
    )(place, pieces, total, first)
    owned, written = pl.pallas_call(
        owned_kernel,
        out_shape=[shape((R, width), BF16), shape((8, LANES), F32)],
        in_specs=[vmem(), later()],
        out_specs=[vmem()] * 2,
        compiler_params=params(),
        cost_estimate=cost(0, 2_000_000),
        name="owned",
    )(scaled, joined)
    returned = lax.all_to_all(back, "fsdp", split_axis=0, concat_axis=0, tiled=True)
    new_momentum, done = pl.pallas_call(
        momentum_kernel,
        out_shape=[shape((count, slots, width), F32), shape((8, LANES), F32)],
        in_specs=[smem()] + [vmem()] * 4 + [later()],
        out_specs=[vmem()] * 2,
        scratch_shapes=[pltpu.VMEM((count, slots, width), F32)],
        compiler_params=params(),
        cost_estimate=cost(0, 4_000_000),
        name="momentum",
    )(lengths, mom, total, first, swap(joined, 1), written)
    chosen = pl.pallas_call(
        select_kernel,
        out_shape=parts,
        in_specs=[smem(), vmem(), later()],
        out_specs=vmem(),
        scratch_shapes=[pltpu.VMEM((slots8, LANES), F32), pltpu.VMEM((rows8, LANES), F32)],
        compiler_params=params(),
        cost_estimate=cost(0, 1_000_000),
        name="select",
    )(owner, returned, done)
    update = pl.pallas_call(
        update_kernel,
        out_shape=shape((count, slots, width), BF16),
        in_specs=[vmem()],
        out_specs=hbm(),
        scratch_shapes=[pltpu.VMEM((count, slots, width), BF16), pltpu.SemaphoreType.DMA((UPDATE_PARTS,))],
        compiler_params=params(),
        cost_estimate=cost(0, 2_000_000),
        name="update",
    )(exchange(chosen))
    return (new_momentum[None], update[None], owned[None])


def solution(mesh):
    in_specs = (P("rep", "fsdp", None, None, None), P("fsdp", None, None, None), P(), P())
    out_specs = (P("fsdp", None, None, None), P("fsdp", None, None, None), P("fsdp", None, None))
    return jax.shard_map(body, mesh=mesh, in_specs=in_specs, out_specs=out_specs, check_vma=False)
```
